32 devices in a mesh: groups: 2 (over y), wide: 4 (over z), trans: 2 (over x), sub: 2 (over core).
Axes of the slice: x: 2, y: 2, z: 4, core: 2. Of those that a mesh axis runs over, the one named last changes fastest.
Arguments:
- start_vectors: float32 [24, 32, 16, 256], P(None, ('groups', 'wide'), ('trans', 'sub')), parts along dimension 1, may hold values from -6 to 6
- hopping: bfloat16 [9, 256, 256], replicated, may hold values from -0.0625 to 0.0625
- pairing: bfloat16 [5, 256, 256], replicated, may hold values from -0.0625 to 0.0625
- onsite: bfloat16 [3, 256, 256], replicated, may hold values from -0.125 to 0.125
- region: int32 [32, 16], P(('groups', 'wide'), ('trans', 'sub')), parts along dimension 0, may hold values from 0 to 2
Outputs:
- cheb_last: float32 [24, 32, 16, 256], P(None, ('groups', 'wide'), ('trans', 'sub')), parts along dimension 1
- cheb_before: float32 [24, 32, 16, 256], P(None, ('groups', 'wide'), ('trans', 'sub')), parts along dimension 1
The draws below stay inside these ranges and needn't reach their ends.
There are 2 independent parts, one for each index of `groups`. The reference program is written for one: setup_inputs(seed, part) draws one part's arguments, and reference() takes and returns one part's arrays. A program takes and returns all parts, laid end to end along the dimension named above; an argument that names none is the same for every part. Nothing has to cross between parts.
All inputs are finite; a program needn't handle non-finite values.
Results may differ from the reference program's by a relative error of at most 0.0046.
Values may be sent and summed in bfloat16 or wider, within the bound.
A program may use at most 64 MiB of HBM per device.

```python
import jax
import jax.numpy as jnp
from jax import lax

B = 256
NV = 24
NREG = 3
ITERS = 4
NXB = 16
NYB = 16


def plant(entries, stream_key, smallest, high):
    longest = entries.shape.index(max(entries.shape))
    spots = []
    for shift in (0, 1):
        where = [jax.random.randint(jax.random.fold_in(stream_key, axis), (), 0, length) for axis, length in enumerate(entries.shape)]
        where[longest] = (where[longest] + shift) % entries.shape[longest]
        spots.append(tuple(where))
    return entries.at[spots[0]].set(smallest).at[spots[1]].set(high)


def steps_of(stream_key, extent, cuts, smallest, top_value):
    gain = 1.0
    for position, shards_of in cuts:
        steps = jax.random.uniform(jax.random.fold_in(jax.random.fold_in(stream_key, 6), position), (shards_of,), jnp.float32, smallest / len(cuts), top_value / len(cuts))
        gain = gain * jnp.repeat(jnp.exp(steps), extent[position] // shards_of).reshape((-1,) + (1,) * (len(extent) - 1 - position))
    return gain


def normal_values(key, extent, deviation, limit, pieces=(), held_as=jnp.bfloat16):
    values = deviation * jax.random.normal(key, extent, jnp.float32)
    if pieces:
        values = values * steps_of(key, extent, pieces, -0.22, 0.18)
    return jnp.clip(values, -limit, limit).astype(held_as)


def setup_inputs(seed: int = 0, part: int = 0) -> dict:
    key_list = jax.random.split(jax.random.key(seed), 6)
    part_splits = jax.random.split(jax.random.fold_in(key_list[5], part), 6)
    start_vectors = normal_values(part_splits[0], (NV, NXB, NYB, B), 1.0, 6.0, ((1, 4), (2, 4)), jnp.float32)
    hopping = normal_values(key_list[1], (9, B, B), (32 * B) ** -0.5, 0.0625)
    pairing = normal_values(key_list[2], (5, B, B), (32 * B) ** -0.5, 0.0625)
    onsite = normal_values(key_list[3], (NREG, B, B), (8 * B) ** -0.5, 0.125)
    region = plant(jax.random.randint(part_splits[4], (NXB, NYB), 0, NREG), jax.random.fold_in(part_splits[4], 1), 0, NREG - 1).astype(jnp.int32)
    return dict(start_vectors=start_vectors, hopping=hopping, pairing=pairing, onsite=onsite, region=region)


HOP_OFFSETS = [(-1, -1), (-1, 0), (-1, 1), (0, -1), (0, 0), (0, 1), (1, -1), (1, 0), (1, 1)]
PAIR_OFFSETS = [(0, 0), (1, 0), (-1, 0), (0, 1), (0, -1)]


def block_product(slab, matrix):
    return jnp.einsum('vxyb,bc->vxyc', slab.astype(jnp.float32), matrix.astype(jnp.float32))


def pad_reflect(field, other):
    extended = jnp.concatenate([jnp.zeros_like(field[:, :1]), field, other[:, -1:]], axis=1)
    return jnp.pad(extended, ((0, 0), (0, 0), (1, 1), (0, 0)))


def window(padded, shift_x, shift_y, count_x, count_y):
    return padded[:, 1 + shift_x:1 + shift_x + count_x, 1 + shift_y:1 + shift_y + count_y, :]


def normal_part(field, padded, regions, hopping, onsite):
    count_x, count_y = field.shape[1], field.shape[2]
    total = jnp.zeros(field.shape, jnp.float32)
    for index, (shift_x, shift_y) in enumerate(HOP_OFFSETS):
        total = total + block_product(window(padded, shift_x, shift_y, count_x, count_y), hopping[index])
    for kind in range(NREG):
        chosen = (regions == kind).astype(field.dtype)[None, :, :, None]
        total = total + block_product(field * chosen, onsite[kind])
    return total


def apply_hamiltonian(rounded, hopping, pairing, onsite, region):
    half_size = NXB // 2
    electrons = rounded[:, :half_size]
    holes = jnp.flip(rounded[:, half_size:], 1)
    region_e = region[:half_size]
    region_h = jnp.flip(region[half_size:], 0)
    padded_e = pad_reflect(electrons, holes)
    padded_h = pad_reflect(holes, electrons)
    count_x, count_y = electrons.shape[1], electrons.shape[2]
    pair_e = jnp.zeros(electrons.shape, jnp.float32)
    pair_h = jnp.zeros(electrons.shape, jnp.float32)
    for index, (shift_x, shift_y) in enumerate(PAIR_OFFSETS):
        pair_e = pair_e + block_product(window(padded_h, shift_x, shift_y, count_x, count_y), pairing[index])
        pair_h = pair_h + block_product(window(padded_e, -shift_x, -shift_y, count_x, count_y), pairing[index].T)
    new_e = normal_part(electrons, padded_e, region_e, hopping, onsite) + pair_e
    new_h = pair_h - normal_part(holes, padded_h, region_h, hopping, onsite)
    return jnp.concatenate([new_e, jnp.flip(new_h, 1)], axis=1)


def reference(start_vectors, hopping, pairing, onsite, region):
    previous = start_vectors
    rounded = lax.optimization_barrier(start_vectors.astype(jnp.bfloat16))
    current = apply_hamiltonian(rounded, hopping, pairing, onsite, region)
    for step in range(ITERS - 1):
        rounded = lax.optimization_barrier(current.astype(jnp.bfloat16))
        following = 2.0 * apply_hamiltonian(rounded, hopping, pairing, onsite, region) - previous
        previous = current
        current = following
    return current, previous
```

```python
import functools

import jax
import jax.numpy as jnp
from jax import lax
from jax.experimental import pallas as pl
from jax.experimental.pallas import tpu as pltpu
from jax.sharding import PartitionSpec as P

MESH = pl.DeviceIdType.MESH

ITERS = 4


HOP_OFFSETS = [(-1, -1), (-1, 0), (-1, 1), (0, -1), (0, 0), (0, 1), (1, -1), (1, 0), (1, 1)]
PAIR_OFFSETS = [(0, 0), (1, 0), (-1, 0), (0, 1), (0, -1)]


def with_halo(array, sides, width):
    for axis, dim in sides:
        size, length = (lax.axis_size(axis), array.shape[dim])
        up = [(i, (i + 1) % size) for i in range(size - 1)]
        down = [(j, i) for i, j in up]
        last = lax.slice_in_dim(array, length - width, length, axis=dim)
        leading = lax.slice_in_dim(array, 0, width, axis=dim)
        before = lax.ppermute(last, axis, up)
        after = lax.ppermute(leading, axis, down)
        array = jnp.concatenate([before, array, after], axis=dim)
    return array


def swapped(value, axis, bit):
    mask = 2**bit
    pairs = [(source, source ^ mask) for source in range(lax.axis_size(axis))]
    return lax.ppermute(value, axis, pairs)


def block_product(slab, matrix):
    return jnp.einsum("vxyb,bc->vxyc", slab, matrix, preferred_element_type=jnp.float32)


def shards(start_vectors, hopping, pairing, onsite, region):
    vectors, count_x, count_y, orbitals = start_vectors.shape
    wide_index = lax.axis_index("wide")
    wide_count = lax.axis_size("wide")
    half_size = wide_count // 2
    bit_count = wide_count.bit_length() - 1
    electron = wide_index < half_size
    sector_sign = jnp.where(electron, 1, -1).astype(jnp.int32)
    sector_scale = jnp.where(electron, 1.0, -1.0).astype(jnp.float32)
    pair_used = jnp.where(electron, pairing, jnp.swapaxes(pairing, 1, 2))
    kinds = jnp.arange(onsite.shape[0], dtype=jnp.int32)
    chosen = (region[None, :, :] == kinds[:, None, None]).astype(jnp.bfloat16)
    onsite_blocks = jnp.sum(chosen[:, :, :, None, None] * onsite[:, None, None, :, :], axis=0)
    anchor = jnp.int32(0)

    def window(padded, start_x, start_y):
        starts = (anchor, jnp.asarray(start_x, jnp.int32), jnp.asarray(start_y, jnp.int32), anchor)
        return lax.dynamic_slice(padded, starts, (vectors, count_x, count_y, orbitals))

    def apply_hamiltonian(rounded):
        padded = with_halo(rounded, (("wide", 1), (("trans", "sub"), 2)), 1)
        received = padded
        for bit_index in range(bit_count):
            received = swapped(received, "wide", bit_index)
        partner = jnp.flip(received, 1)
        normal = jnp.einsum(
            "vxyb,xybc->vxyc", rounded, onsite_blocks, preferred_element_type=jnp.float32
        )
        for offset_index, (shift_x, shift_y) in enumerate(HOP_OFFSETS):
            slab = window(padded, 1 + sector_sign * shift_x, 1 + shift_y)
            normal = normal + block_product(slab, hopping[offset_index])
        paired = jnp.zeros(rounded.shape, jnp.float32)
        for offset_index, (shift_x, shift_y) in enumerate(PAIR_OFFSETS):
            slab = window(partner, 1 + shift_x, 1 + sector_sign * shift_y)
            paired = paired + block_product(slab, pair_used[offset_index])
        return sector_scale * normal + paired

    previous = start_vectors
    current = apply_hamiltonian(start_vectors.astype(jnp.bfloat16))
    for step in range(ITERS - 1):
        following = 2.0 * apply_hamiltonian(current.astype(jnp.bfloat16)) - previous
        previous = current
        current = following
    return (current, previous)


CHIP_VECTORS = 3
SLOTS = 2


def home_row(out_row, half, rows, wide_len, row_len):
    x = out_row // (2 * rows)
    sector = (out_row // rows) % 2
    y = out_row % rows
    column = jnp.where(sector == 0, x, 2 * half - 1 - x)
    domains = rows // row_len
    return ((column // wide_len) * domains + y // row_len) * (wide_len * row_len) + (column % wide_len) * row_len + y % row_len


def vector_kernel(
    sizes, r0, reg, hop, pair, onsite, out,
    recv, regs, wn, wp, wpt, buf, previous, current, stage, kind,
    send_sem, recv_sem, rsend_sem, rrecv_sem, osend_sem, orecv_sem, weight_sem,
):
    wide, trans, sub, wide_len, row_len = sizes
    domains = trans * sub
    sources = wide * domains
    half = wide * wide_len // 2
    rows = domains * row_len
    cells = 2 * half * rows
    count, orbitals = r0.shape[0], r0.shape[2]
    total = SLOTS * cells
    group = lax.axis_index("groups")
    z, t, c = lax.axis_index("wide"), lax.axis_index("trans"), lax.axis_index("sub")
    me = z * domains + t * sub + c
    my_first = (z * trans + t) * CHIP_VECTORS + c * SLOTS
    my_slots = SLOTS - c

    def device(index):
        return (group, index // domains, (index % domains) // sub, index % sub)

    def owner(v):
        chip, place = v // CHIP_VECTORS, v % CHIP_VECTORS
        return chip * sub + place // SLOTS, place % SLOTS

    loads = [
        pltpu.make_async_copy(hop, wn.at[pl.ds(0, 9)], weight_sem.at[0]),
        pltpu.make_async_copy(onsite, wn.at[pl.ds(9, 3)], weight_sem.at[1]),
        pltpu.make_async_copy(pair, wp, weight_sem.at[2]),
    ]
    for load in loads:
        load.start()

    barrier = pltpu.get_barrier_semaphore()

    def greet(j, carry):
        pl.semaphore_signal(barrier, inc=1, device_id=device((me + j) % sources), device_id_type=MESH)
        return carry

    lax.fori_loop(1, sources, greet, 0)
    pl.semaphore_wait(barrier, sources - 1)

    def region_copy(to, frm):
        return pltpu.make_async_remote_copy(
            src_ref=reg, dst_ref=regs.at[frm], send_sem=rsend_sem.at[to], recv_sem=rrecv_sem.at[frm],
            device_id=device(to), device_id_type=MESH,
        )

    def vector_copy(v, frm):
        to, slot = owner(v)
        return pltpu.make_async_remote_copy(
            src_ref=r0.at[v], dst_ref=recv.at[slot, frm], send_sem=send_sem.at[v], recv_sem=recv_sem.at[slot, frm],
            device_id=device(to), device_id_type=MESH,
        )

    def send_vector(j, carry):
        v = (my_first + j + count // 2) % count

        @pl.when(owner(v)[0] != me)
        def _():
            vector_copy(v, me).start()

        return carry

    lax.fori_loop(0, count, send_vector, 0)

    def send_region(j, carry):
        region_copy((me + j) % sources, me).start()
        return carry

    lax.fori_loop(1, sources, send_region, 0)

    regs[me] = reg[...]
    recv[0, me] = r0[my_first]

    @pl.when(c == 0)
    def _():
        recv[1, me] = r0[my_first + 1]

    @pl.when(c != 0)
    def _():
        recv[1] = jnp.zeros(recv.shape[1:], recv.dtype)

    buf[:, 0] = jnp.zeros((3,) + buf.shape[2:], buf.dtype)
    previous[...] = jnp.zeros(previous.shape, jnp.float32)
    for load in loads:
        load.wait()
    for k in range(5):
        wpt[k] = wp[k].T

    lattice = lax.broadcasted_iota(jnp.int32, (cells, cells), 0)
    home = lax.broadcasted_iota(jnp.int32, (cells, cells), 1)
    to_lattice = (home_row(lattice, half, rows, wide_len, row_len) == home).astype(jnp.bfloat16)

    def wait_region(j, carry):
        frm = (me + j) % sources
        region_copy(frm, frm).wait_recv()
        return carry

    def wait_vector(j, carry):
        frm = (me + j) % sources
        for slot in range(SLOTS):

            @pl.when(slot < my_slots)
            def _():
                vector_copy(my_first + slot, frm).wait_recv()

        return carry

    lax.fori_loop(1, sources, wait_region, 0)
    per = wide_len * row_len
    spots = lax.broadcasted_iota(jnp.int32, (cells, sources), 0)
    spots = home_row(spots, half, rows, wide_len, row_len)
    picks = (spots // per == lax.broadcasted_iota(jnp.int32, (cells, sources), 1)).astype(jnp.float32)
    spread = jnp.dot(picks, regs[...].reshape(sources, reg.shape[1]), preferred_element_type=jnp.float32)
    lanes = lax.broadcasted_iota(jnp.int32, spread.shape, 1)
    places = lax.broadcasted_iota(jnp.int32, spread.shape, 0)
    places = home_row(places, half, rows, wide_len, row_len) % per
    kinds = jnp.sum(jnp.where(lanes == places, spread, 0.0), axis=1, keepdims=True)
    kinds = jnp.broadcast_to(kinds, (cells, orbitals)).reshape(2 * half, 1, rows, orbitals)
    kinds = jnp.concatenate([kinds] * SLOTS, axis=1)
    kind[...] = kinds.reshape(total, orbitals).astype(jnp.bfloat16)
    lax.fori_loop(1, sources, wait_vector, 0)

    parts = []
    for slot in range(SLOTS):
        part = jnp.dot(to_lattice, recv[slot].reshape(cells, orbitals), preferred_element_type=jnp.float32)
        parts.append(part.reshape(half * 2, 1, rows, orbitals))
    current[...] = jnp.concatenate(parts, axis=1).reshape(total, orbitals)

    def store_fields():
        field = current[...]
        y = lax.broadcasted_iota(jnp.int32, field.shape, 0) % rows
        below = jnp.where(y == 0, 0.0, pltpu.roll(field, 1, 0))
        above = jnp.where(y == rows - 1, 0.0, pltpu.roll(field, total - 1, 0))
        for index, value in enumerate((below, field, above)):
            value = value.astype(jnp.bfloat16).reshape((half, 2, SLOTS * rows, orbitals))
            buf[index, 1 : half + 1] = value
            buf[index, half + 1, 0] = value[half - 1, 1]
            buf[index, half + 1, 1] = value[half - 1, 0]

    def out_copy(which, slot, to, v):
        return pltpu.make_async_remote_copy(
            src_ref=stage.at[which, slot, to], dst_ref=out.at[which, v],
            send_sem=osend_sem.at[which, slot, to], recv_sem=orecv_sem.at[which, v],
            device_id=device(to), device_id_type=MESH,
        )

    def send_home(which, values):
        values = values.reshape(2 * half, SLOTS, rows, orbitals)
        for slot in range(SLOTS):
            part = lax.dot_general(
                to_lattice, values[:, slot].reshape(cells, orbitals), (((0,), (0,)), ((), ())),
                preferred_element_type=jnp.float32,
            )
            stage[which, slot] = part.astype(jnp.bfloat16).reshape(stage.shape[2:])

            @pl.when(slot < my_slots)
            def _():
                out[which, my_first + slot] = stage[which, slot, me]

        def send(j, carry):
            to = (me + j) % sources
            for slot in range(SLOTS):

                @pl.when(slot < my_slots)
                def _():
                    out_copy(which, slot, to, my_first + slot).start()

            return carry

        lax.fori_loop(1, sources, send, 0)

    def slab(a, b):
        return buf[b + 1, 1 + a : 1 + a + half].reshape(total, orbitals)

    def sector_slab(a, b, sector):
        return buf[b + 1, 1 + a : 1 + a + half, sector].reshape(total // 2, orbitals)

    def apply(carry_scale, carry_old):
        normal = jnp.dot(slab(*HOP_OFFSETS[0]), wn[0], preferred_element_type=jnp.float32)
        for k in range(1, 9):
            normal = normal + jnp.dot(slab(*HOP_OFFSETS[k]), wn[k], preferred_element_type=jnp.float32)
        for r in range(3):
            chosen = jnp.where(kind[...] == r, slab(0, 0), jnp.zeros((), jnp.bfloat16))
            normal = normal + jnp.dot(chosen, wn[9 + r], preferred_element_type=jnp.float32)
        to_e = jnp.zeros((total // 2, orbitals), jnp.float32)
        to_h = jnp.zeros((total // 2, orbitals), jnp.float32)
        for k, (a, b) in enumerate(PAIR_OFFSETS):
            to_e = to_e + jnp.dot(sector_slab(a, b, 1), wp[k], preferred_element_type=jnp.float32)
            to_h = to_h + jnp.dot(sector_slab(-a, -b, 0), wpt[k], preferred_element_type=jnp.float32)
        shape = (half, SLOTS * rows, orbitals)
        normal = normal.reshape(half, 2, SLOTS * rows, orbitals)
        new_e = normal[:, 0] + to_e.reshape(shape)
        new_h = to_h.reshape(shape) - normal[:, 1]
        new = jnp.stack([new_e, new_h], axis=1).reshape(total, orbitals)
        new = carry_scale * new - carry_old * previous[...]
        previous[...] = current[...]
        current[...] = new

    def step(it, carry):
        store_fields()

        @pl.when(it == ITERS - 1)
        def _():
            send_home(1, slab(0, 0))

        first = it == 0
        apply(jnp.where(first, 1.0, 2.0), jnp.where(first, 0.0, 1.0))
        return carry

    lax.fori_loop(0, ITERS, step, 0)
    send_home(0, current[...].astype(jnp.bfloat16))

    def finish_out(v, carry):
        @pl.when(owner(v)[0] != me)
        def _():
            vector_copy(v, me).wait_send()
            for which in range(2):
                out_copy(which, 0, owner(v)[0], v).wait_recv()

        return carry

    lax.fori_loop(0, count, finish_out, 0)

    def finish_sends(j, carry):
        to = (me + j) % sources
        region_copy(to, me).wait_send()
        for slot in range(SLOTS):

            @pl.when(slot < my_slots)
            def _():
                for which in range(2):
                    out_copy(which, slot, to, my_first + slot).wait_send()

        return carry

    lax.fori_loop(1, sources, finish_sends, 0)


def by_vectors(sizes, start_vectors, hopping, pairing, onsite, region):
    wide, trans, sub = sizes
    count, wide_len, row_len, orbitals = start_vectors.shape
    domains = trans * sub
    sources, per = wide * domains, wide_len * row_len
    half, rows = wide * wide_len // 2, domains * row_len
    cells = 2 * half * rows
    total = SLOTS * cells
    rounded = start_vectors.reshape(count, per, orbitals).astype(jnp.bfloat16)
    regions = jnp.pad(region.reshape(1, per).astype(jnp.float32), ((0, 0), (0, 128 - per)))
    vmem = pl.BlockSpec(memory_space=pltpu.VMEM)
    hbm = pl.BlockSpec(memory_space=pl.ANY)
    bf16, f32 = jnp.bfloat16, jnp.float32
    dma = pltpu.SemaphoreType.DMA
    out = pl.pallas_call(
        functools.partial(vector_kernel, sizes + (wide_len, row_len)),
        out_shape=jax.ShapeDtypeStruct((2, count, per, orbitals), bf16),
        in_specs=[vmem, vmem, hbm, hbm, hbm],
        out_specs=vmem,
        scratch_shapes=[
            pltpu.VMEM((SLOTS, sources, per, orbitals), bf16),
            pltpu.VMEM((sources, 1, 128), f32),
            pltpu.VMEM((12, orbitals, orbitals), bf16),
            pltpu.VMEM((5, orbitals, orbitals), bf16),
            pltpu.VMEM((5, orbitals, orbitals), bf16),
            pltpu.VMEM((3, half + 2, 2, SLOTS * rows, orbitals), bf16),
            pltpu.VMEM((total, orbitals), f32),
            pltpu.VMEM((total, orbitals), f32),
            pltpu.VMEM((2, SLOTS, sources, per, orbitals), bf16),
            pltpu.VMEM((total, orbitals), bf16),
            dma((count,)),
            dma((SLOTS, sources)),
            dma((sources,)),
            dma((sources,)),
            dma((2, SLOTS, sources)),
            dma((2, count)),
            dma((3,)),
        ],
        compiler_params=pltpu.CompilerParams(
            collective_id=0, has_side_effects=True, vmem_limit_bytes=40 * 2**20
        ),
    )(rounded, regions, hopping, pairing, onsite)
    wanted = out.astype(f32).reshape((2,) + start_vectors.shape)
    return wanted[0], wanted[1]


def solution(mesh):
    sizes = (mesh.shape["wide"], mesh.shape["trans"], mesh.shape["sub"])
    per_device = shards
    if sizes == (4, 2, 2):
        per_device = functools.partial(by_vectors, sizes)
    in_specs = (
        P(None, ("groups", "wide"), ("trans", "sub"), None),
        P(),
        P(),
        P(),
        P(("groups", "wide"), ("trans", "sub")),
    )
    out_specs = (
        P(None, ("groups", "wide"), ("trans", "sub"), None),
        P(None, ("groups", "wide"), ("trans", "sub"), None),
    )
    return jax.shard_map(per_device, mesh=mesh, in_specs=in_specs, out_specs=out_specs, check_vma=False)
```

```python
import functools

import jax
import jax.numpy as jnp
from jax import lax
from jax.experimental import pallas as pl
from jax.experimental.pallas import tpu as pltpu
from jax.sharding import PartitionSpec as P

MESH = pl.DeviceIdType.MESH

ITERS = 4


HOP_OFFSETS = [(-1, -1), (-1, 0), (-1, 1), (0, -1), (0, 0), (0, 1), (1, -1), (1, 0), (1, 1)]
PAIR_OFFSETS = [(0, 0), (1, 0), (-1, 0), (0, 1), (0, -1)]


def with_halo(array, sides, width):
    for axis, dim in sides:
        size, length = (lax.axis_size(axis), array.shape[dim])
        up = [(i, (i + 1) % size) for i in range(size - 1)]
        down = [(j, i) for i, j in up]
        last = lax.slice_in_dim(array, length - width, length, axis=dim)
        leading = lax.slice_in_dim(array, 0, width, axis=dim)
        before = lax.ppermute(last, axis, up)
        after = lax.ppermute(leading, axis, down)
        array = jnp.concatenate([before, array, after], axis=dim)
    return array


def swapped(value, axis, bit):
    mask = 2**bit
    pairs = [(source, source ^ mask) for source in range(lax.axis_size(axis))]
    return lax.ppermute(value, axis, pairs)


def block_product(slab, matrix):
    return jnp.einsum("vxyb,bc->vxyc", slab, matrix, preferred_element_type=jnp.float32)


def shards(start_vectors, hopping, pairing, onsite, region):
    vectors, count_x, count_y, orbitals = start_vectors.shape
    wide_index = lax.axis_index("wide")
    wide_count = lax.axis_size("wide")
    half_size = wide_count // 2
    bit_count = wide_count.bit_length() - 1
    electron = wide_index < half_size
    sector_sign = jnp.where(electron, 1, -1).astype(jnp.int32)
    sector_scale = jnp.where(electron, 1.0, -1.0).astype(jnp.float32)
    pair_used = jnp.where(electron, pairing, jnp.swapaxes(pairing, 1, 2))
    kinds = jnp.arange(onsite.shape[0], dtype=jnp.int32)
    chosen = (region[None, :, :] == kinds[:, None, None]).astype(jnp.bfloat16)
    onsite_blocks = jnp.sum(chosen[:, :, :, None, None] * onsite[:, None, None, :, :], axis=0)
    anchor = jnp.int32(0)

    def window(padded, start_x, start_y):
        starts = (anchor, jnp.asarray(start_x, jnp.int32), jnp.asarray(start_y, jnp.int32), anchor)
        return lax.dynamic_slice(padded, starts, (vectors, count_x, count_y, orbitals))

    def apply_hamiltonian(rounded):
        padded = with_halo(rounded, (("wide", 1), (("trans", "sub"), 2)), 1)
        received = padded
        for bit_index in range(bit_count):
            received = swapped(received, "wide", bit_index)
        partner = jnp.flip(received, 1)
        normal = jnp.einsum(
            "vxyb,xybc->vxyc", rounded, onsite_blocks, preferred_element_type=jnp.float32
        )
        for offset_index, (shift_x, shift_y) in enumerate(HOP_OFFSETS):
            slab = window(padded, 1 + sector_sign * shift_x, 1 + shift_y)
            normal = normal + block_product(slab, hopping[offset_index])
        paired = jnp.zeros(rounded.shape, jnp.float32)
        for offset_index, (shift_x, shift_y) in enumerate(PAIR_OFFSETS):
            slab = window(partner, 1 + shift_x, 1 + sector_sign * shift_y)
            paired = paired + block_product(slab, pair_used[offset_index])
        return sector_scale * normal + paired

    previous = start_vectors
    current = apply_hamiltonian(start_vectors.astype(jnp.bfloat16))
    for step in range(ITERS - 1):
        following = 2.0 * apply_hamiltonian(current.astype(jnp.bfloat16)) - previous
        previous = current
        current = following
    return (current, previous)


CHIP_VECTORS = 3
SLOTS = 2


def home_row(out_row, half, rows, wide_len, row_len):
    x = out_row // (2 * rows)
    sector = (out_row // rows) % 2
    y = out_row % rows
    column = jnp.where(sector == 0, x, 2 * half - 1 - x)
    domains = rows // row_len
    return ((column // wide_len) * domains + y // row_len) * (wide_len * row_len) + (column % wide_len) * row_len + y % row_len


def vector_kernel(
    sizes, start, region, hop, pair, onsite, out,
    raw, wide_raw, r0, reg_raw, reg, recv, regs, wn, wp, wpt, buf, previous, current, stage, mask,
    send_sem, recv_sem, rsend_sem, rrecv_sem, osend_sem, orecv_sem, weight_sem,
):
    wide, trans, sub, wide_len, row_len = sizes
    domains = trans * sub
    sources = wide * domains
    half = wide * wide_len // 2
    rows = domains * row_len
    cells = 2 * half * rows
    count, orbitals = r0.shape[0], r0.shape[2]
    group = lax.axis_index("groups")
    z, t, c = lax.axis_index("wide"), lax.axis_index("trans"), lax.axis_index("sub")
    me = z * domains + t * sub + c
    my_first = (z * trans + t) * CHIP_VECTORS + c * SLOTS
    my_slots = SLOTS - c

    def device(index):
        return (group, index // domains, (index % domains) // sub, index % sub)

    def owner(v):
        chip, place = v // CHIP_VECTORS, v % CHIP_VECTORS
        return chip * sub + place // SLOTS, place % SLOTS

    barrier = pltpu.get_barrier_semaphore()

    def greet(j, carry):
        pl.semaphore_signal(barrier, inc=1, device_id=device((me + j) % sources), device_id_type=MESH)
        return carry

    lax.fori_loop(1, sources, greet, 0)

    first_load = pltpu.make_async_copy(start, raw, weight_sem.at[3])
    region_load = pltpu.make_async_copy(region, reg_raw, weight_sem.at[4])
    loads = [
        pltpu.make_async_copy(hop, wn.at[pl.ds(0, 9)], weight_sem.at[0]),
        pltpu.make_async_copy(onsite, wn.at[pl.ds(9, 3)], weight_sem.at[1]),
        pltpu.make_async_copy(pair, wp, weight_sem.at[2]),
    ]
    first_load.start()
    region_load.start()
    for load in loads:
        load.start()
    region_load.wait()
    lane = lax.broadcasted_iota(jnp.int32, reg.shape, 1)
    row = jnp.zeros(reg.shape, jnp.float32)
    for xl in range(wide_len):
        for yl in range(row_len):
            value = reg_raw[xl : xl + 1, yl : yl + 1].astype(jnp.float32)
            row = jnp.where(lane == xl * row_len + yl, value, row)
    reg[...] = row
    first_load.wait()
    for xl in range(wide_len):
        wide_raw[:, xl * row_len : (xl + 1) * row_len] = raw[:, xl]
    r0[...] = wide_raw[...].astype(jnp.bfloat16)
    pl.semaphore_wait(barrier, sources - 1)

    def region_copy(to, frm):
        return pltpu.make_async_remote_copy(
            src_ref=reg, dst_ref=regs.at[frm], send_sem=rsend_sem.at[to], recv_sem=rrecv_sem.at[frm],
            device_id=device(to), device_id_type=MESH,
        )

    def vector_copy(v, frm):
        to, slot = owner(v)
        return pltpu.make_async_remote_copy(
            src_ref=r0.at[v], dst_ref=recv.at[slot, frm], send_sem=send_sem.at[v], recv_sem=recv_sem.at[slot, frm],
            device_id=device(to), device_id_type=MESH,
        )

    chips = sources // sub

    def send_vectors(offset):
        def send_vector(j, carry):
            chip = (me // sub + j + chips // 2) % chips
            v = chip * CHIP_VECTORS + offset

            @pl.when(owner(v)[0] != me)
            def _():
                vector_copy(v, me).start()

            return carry

        lax.fori_loop(0, chips, send_vector, 0)

    def send_region(j, carry):
        region_copy((me + j) % sources, me).start()
        return carry

    lax.fori_loop(1, sources, send_region, 0)
    for offset in (0, 2, 1):
        send_vectors(offset)

    regs[me] = reg[...]
    recv[0, me] = r0[my_first]

    @pl.when(c == 0)
    def _():
        recv[1, me] = r0[my_first + 1]

    buf[:, 0] = jnp.zeros((3,) + buf.shape[2:], buf.dtype)
    for load in loads:
        load.wait()
    for k in range(5):
        wpt[k] = wp[k].T

    lattice = lax.broadcasted_iota(jnp.int32, (cells, cells), 0)
    home = lax.broadcasted_iota(jnp.int32, (cells, cells), 1)
    to_lattice = (home_row(lattice, half, rows, wide_len, row_len) == home).astype(jnp.bfloat16)

    def wait_region(j, carry):
        frm = (me + j) % sources
        region_copy(frm, frm).wait_recv()
        return carry

    lax.fori_loop(1, sources, wait_region, 0)
    per = wide_len * row_len
    spots = lax.broadcasted_iota(jnp.int32, (cells, sources), 0)
    spots = home_row(spots, half, rows, wide_len, row_len)
    picks = (spots // per == lax.broadcasted_iota(jnp.int32, (cells, sources), 1)).astype(jnp.float32)
    spread = jnp.dot(picks, regs[...].reshape(sources, reg.shape[1]), preferred_element_type=jnp.float32)
    lanes = lax.broadcasted_iota(jnp.int32, spread.shape, 1)
    places = lax.broadcasted_iota(jnp.int32, spread.shape, 0)
    places = home_row(places, half, rows, wide_len, row_len) % per
    kinds = jnp.sum(jnp.where(lanes == places, spread, 0.0), axis=1, keepdims=True)
    kinds = jnp.broadcast_to(kinds, (cells, orbitals))
    for r in range(3):
        mask[r] = jnp.where(kinds == r, 1.0, 0.0).astype(jnp.bfloat16)

    def store_fields():
        field = current[...]
        y = lax.broadcasted_iota(jnp.int32, field.shape, 0) % rows
        below = jnp.where(y == 0, 0.0, pltpu.roll(field, 1, 0))
        above = jnp.where(y == rows - 1, 0.0, pltpu.roll(field, cells - 1, 0))
        for index, value in enumerate((below, field, above)):
            value = value.astype(jnp.bfloat16).reshape((half, 2, rows, orbitals))
            buf[index, 1 : half + 1] = value
            buf[index, half + 1, 0] = value[half - 1, 1]
            buf[index, half + 1, 1] = value[half - 1, 0]

    def out_copy(which, slot, to, v):
        return pltpu.make_async_remote_copy(
            src_ref=stage.at[which, slot, to], dst_ref=out.at[which, v],
            send_sem=osend_sem.at[which, slot, to], recv_sem=orecv_sem.at[which, v],
            device_id=device(to), device_id_type=MESH,
        )

    def send_home(which, slot, values):
        part = lax.dot_general(
            to_lattice, values, (((0,), (0,)), ((), ())), preferred_element_type=jnp.float32
        )
        stage[which, slot] = part.astype(jnp.bfloat16).reshape(stage.shape[2:])
        out[which, my_first + slot] = stage[which, slot, me]

        def send(j, carry):
            to = (me + j) % sources
            out_copy(which, slot, to, my_first + slot).start()
            return carry

        lax.fori_loop(1, sources, send, 0)

    def slab(a, b):
        return buf[b + 1, 1 + a : 1 + a + half].reshape(cells, orbitals)

    def sector_slab(a, b, sector):
        return buf[b + 1, 1 + a : 1 + a + half, sector].reshape(cells // 2, orbitals)

    def apply(carry_scale, carry_old):
        normal = jnp.dot(slab(*HOP_OFFSETS[0]), wn[0], preferred_element_type=jnp.float32)
        for k in range(1, 9):
            normal = normal + jnp.dot(slab(*HOP_OFFSETS[k]), wn[k], preferred_element_type=jnp.float32)
        for r in range(3):
            chosen = slab(0, 0) * mask[r]
            normal = normal + jnp.dot(chosen, wn[9 + r], preferred_element_type=jnp.float32)
        to_e = jnp.zeros((cells // 2, orbitals), jnp.float32)
        to_h = jnp.zeros((cells // 2, orbitals), jnp.float32)
        for k, (a, b) in enumerate(PAIR_OFFSETS):
            to_e = to_e + jnp.dot(sector_slab(a, b, 1), wp[k], preferred_element_type=jnp.float32)
            to_h = to_h + jnp.dot(sector_slab(-a, -b, 0), wpt[k], preferred_element_type=jnp.float32)
        shape = (half, rows, orbitals)
        normal = normal.reshape(half, 2, rows, orbitals)
        new_e = normal[:, 0] + to_e.reshape(shape)
        new_h = to_h.reshape(shape) - normal[:, 1]
        new = jnp.stack([new_e, new_h], axis=1).reshape(cells, orbitals)
        new = carry_scale * new - carry_old * previous[...]
        previous[...] = current[...]
        current[...] = new

    def run(slot, carry):
        @pl.when(slot < my_slots)
        def _():
            def wait_vector(j, carry):
                vector_copy(my_first + slot, (me + j) % sources).wait_recv()
                return carry

            lax.fori_loop(1, sources, wait_vector, 0)
            current[...] = jnp.dot(
                to_lattice, recv[slot].reshape(cells, orbitals), preferred_element_type=jnp.float32
            )
            previous[...] = jnp.zeros(previous.shape, jnp.float32)

            def step(it, carry):
                store_fields()

                @pl.when(it == ITERS - 1)
                def _():
                    send_home(1, slot, slab(0, 0))

                first = it == 0
                apply(jnp.where(first, 1.0, 2.0), jnp.where(first, 0.0, 1.0))
                return carry

            lax.fori_loop(0, ITERS, step, 0)
            send_home(0, slot, current[...].astype(jnp.bfloat16))

        return carry

    lax.fori_loop(0, SLOTS, run, 0)

    def finish_out(v, carry):
        @pl.when(owner(v)[0] != me)
        def _():
            vector_copy(v, me).wait_send()
            for which in range(2):
                out_copy(which, 0, owner(v)[0], v).wait_recv()

        return carry

    lax.fori_loop(0, count, finish_out, 0)

    def finish_sends(j, carry):
        to = (me + j) % sources
        region_copy(to, me).wait_send()
        for slot in range(SLOTS):

            @pl.when(slot < my_slots)
            def _():
                for which in range(2):
                    out_copy(which, slot, to, my_first + slot).wait_send()

        return carry

    lax.fori_loop(1, sources, finish_sends, 0)


def by_vectors(sizes, start_vectors, hopping, pairing, onsite, region):
    wide, trans, sub = sizes
    count, wide_len, row_len, orbitals = start_vectors.shape
    domains = trans * sub
    sources, per = wide * domains, wide_len * row_len
    half, rows = wide * wide_len // 2, domains * row_len
    cells = 2 * half * rows
    vmem = pl.BlockSpec(memory_space=pltpu.VMEM)
    hbm = pl.BlockSpec(memory_space=pl.ANY)
    bf16, f32 = jnp.bfloat16, jnp.float32
    dma = pltpu.SemaphoreType.DMA
    out = pl.pallas_call(
        functools.partial(vector_kernel, sizes + (wide_len, row_len)),
        out_shape=jax.ShapeDtypeStruct((2, count, per, orbitals), bf16),
        in_specs=[hbm] * 5,
        out_specs=vmem,
        scratch_shapes=[
            pltpu.VMEM(start_vectors.shape, f32),
            pltpu.VMEM((count, per, orbitals), f32),
            pltpu.VMEM((count, per, orbitals), bf16),
            pltpu.VMEM(region.shape, region.dtype),
            pltpu.VMEM((1, 128), f32),
            pltpu.VMEM((SLOTS, sources, per, orbitals), bf16),
            pltpu.VMEM((sources, 1, 128), f32),
            pltpu.VMEM((12, orbitals, orbitals), bf16),
            pltpu.VMEM((5, orbitals, orbitals), bf16),
            pltpu.VMEM((5, orbitals, orbitals), bf16),
            pltpu.VMEM((3, half + 2, 2, rows, orbitals), bf16),
            pltpu.VMEM((cells, orbitals), f32),
            pltpu.VMEM((cells, orbitals), f32),
            pltpu.VMEM((2, SLOTS, sources, per, orbitals), bf16),
            pltpu.VMEM((3, cells, orbitals), bf16),
            dma((count,)),
            dma((SLOTS, sources)),
            dma((sources,)),
            dma((sources,)),
            dma((2, SLOTS, sources)),
            dma((2, count)),
            dma((5,)),
        ],
        compiler_params=pltpu.CompilerParams(
            collective_id=0, has_side_effects=True, vmem_limit_bytes=60 * 2**20
        ),
    )(start_vectors, region, hopping, pairing, onsite)
    wanted = out.astype(f32).reshape((2,) + start_vectors.shape)
    return wanted[0], wanted[1]


def solution(mesh):
    sizes = (mesh.shape["wide"], mesh.shape["trans"], mesh.shape["sub"])
    per_device = shards
    if sizes == (4, 2, 2):
        per_device = functools.partial(by_vectors, sizes)
    in_specs = (
        P(None, ("groups", "wide"), ("trans", "sub"), None),
        P(),
        P(),
        P(),
        P(("groups", "wide"), ("trans", "sub")),
    )
    out_specs = (
        P(None, ("groups", "wide"), ("trans", "sub"), None),
        P(None, ("groups", "wide"), ("trans", "sub"), None),
    )
    return jax.shard_map(per_device, mesh=mesh, in_specs=in_specs, out_specs=out_specs, check_vma=False)
```

```python
import functools

import jax
import jax.numpy as jnp
from jax import lax
from jax.experimental import pallas as pl
from jax.experimental.pallas import tpu as pltpu
from jax.sharding import PartitionSpec as P

MESH = pl.DeviceIdType.MESH

ITERS = 4


HOP_OFFSETS = [(-1, -1), (-1, 0), (-1, 1), (0, -1), (0, 0), (0, 1), (1, -1), (1, 0), (1, 1)]
PAIR_OFFSETS = [(0, 0), (1, 0), (-1, 0), (0, 1), (0, -1)]


def with_halo(array, sides, width):
    for axis, dim in sides:
        size, length = (lax.axis_size(axis), array.shape[dim])
        up = [(i, (i + 1) % size) for i in range(size - 1)]
        down = [(j, i) for i, j in up]
        last = lax.slice_in_dim(array, length - width, length, axis=dim)
        leading = lax.slice_in_dim(array, 0, width, axis=dim)
        before = lax.ppermute(last, axis, up)
        after = lax.ppermute(leading, axis, down)
        array = jnp.concatenate([before, array, after], axis=dim)
    return array


def swapped(value, axis, bit):
    mask = 2**bit
    pairs = [(source, source ^ mask) for source in range(lax.axis_size(axis))]
    return lax.ppermute(value, axis, pairs)


def block_product(slab, matrix):
    return jnp.einsum("vxyb,bc->vxyc", slab, matrix, preferred_element_type=jnp.float32)


def shards(start_vectors, hopping, pairing, onsite, region):
    vectors, count_x, count_y, orbitals = start_vectors.shape
    wide_index = lax.axis_index("wide")
    wide_count = lax.axis_size("wide")
    half_size = wide_count // 2
    bit_count = wide_count.bit_length() - 1
    electron = wide_index < half_size
    sector_sign = jnp.where(electron, 1, -1).astype(jnp.int32)
    sector_scale = jnp.where(electron, 1.0, -1.0).astype(jnp.float32)
    pair_used = jnp.where(electron, pairing, jnp.swapaxes(pairing, 1, 2))
    kinds = jnp.arange(onsite.shape[0], dtype=jnp.int32)
    chosen = (region[None, :, :] == kinds[:, None, None]).astype(jnp.bfloat16)
    onsite_blocks = jnp.sum(chosen[:, :, :, None, None] * onsite[:, None, None, :, :], axis=0)
    anchor = jnp.int32(0)

    def window(padded, start_x, start_y):
        starts = (anchor, jnp.asarray(start_x, jnp.int32), jnp.asarray(start_y, jnp.int32), anchor)
        return lax.dynamic_slice(padded, starts, (vectors, count_x, count_y, orbitals))

    def apply_hamiltonian(rounded):
        padded = with_halo(rounded, (("wide", 1), (("trans", "sub"), 2)), 1)
        received = padded
        for bit_index in range(bit_count):
            received = swapped(received, "wide", bit_index)
        partner = jnp.flip(received, 1)
        normal = jnp.einsum(
            "vxyb,xybc->vxyc", rounded, onsite_blocks, preferred_element_type=jnp.float32
        )
        for offset_index, (shift_x, shift_y) in enumerate(HOP_OFFSETS):
            slab = window(padded, 1 + sector_sign * shift_x, 1 + shift_y)
            normal = normal + block_product(slab, hopping[offset_index])
        paired = jnp.zeros(rounded.shape, jnp.float32)
        for offset_index, (shift_x, shift_y) in enumerate(PAIR_OFFSETS):
            slab = window(partner, 1 + shift_x, 1 + sector_sign * shift_y)
            paired = paired + block_product(slab, pair_used[offset_index])
        return sector_scale * normal + paired

    previous = start_vectors
    current = apply_hamiltonian(start_vectors.astype(jnp.bfloat16))
    for step in range(ITERS - 1):
        following = 2.0 * apply_hamiltonian(current.astype(jnp.bfloat16)) - previous
        previous = current
        current = following
    return (current, previous)


CHIP_VECTORS = 3
SLOTS = 2


def home_row(out_row, half, rows, wide_len, row_len):
    x = out_row // (2 * rows)
    sector = (out_row // rows) % 2
    y = out_row % rows
    column = jnp.where(sector == 0, x, 2 * half - 1 - x)
    domains = rows // row_len
    return ((column // wide_len) * domains + y // row_len) * (wide_len * row_len) + (column % wide_len) * row_len + y % row_len


def vector_kernel(
    sizes, start, region, hop, pair, onsite, last, before,
    raw, wide_raw, out, r0, reg_raw, reg, recv, regs, wn, wp, wpt, buf, previous, current, stage, mask,
    send_sem, recv_sem, rsend_sem, rrecv_sem, osend_sem, orecv_sem, weight_sem,
):
    wide, trans, sub, wide_len, row_len = sizes
    domains = trans * sub
    sources = wide * domains
    half = wide * wide_len // 2
    rows = domains * row_len
    cells = 2 * half * rows
    count, orbitals = r0.shape[0], r0.shape[2]
    group = lax.axis_index("groups")
    z, t, c = lax.axis_index("wide"), lax.axis_index("trans"), lax.axis_index("sub")
    me = z * domains + t * sub + c
    my_first = (z * trans + t) * CHIP_VECTORS + c * SLOTS
    my_slots = SLOTS - c

    peers = []
    for dz in sorted(range(wide), key=lambda dz: -min(dz, wide - dz)):
        for dt in range(trans):
            for dc in range(sub):
                if dz or dt or dc:
                    to_z, to_t, to_c = lax.rem(z + dz, wide), lax.rem(t + dt, trans), lax.rem(c + dc, sub)
                    peers.append(((group, to_z, to_t, to_c), to_z * domains + to_t * sub + to_c))

    barrier = pltpu.get_barrier_semaphore()

    for place, index in peers:
        pl.semaphore_signal(barrier, inc=1, device_id=place, device_id_type=MESH)

    first_load = pltpu.make_async_copy(start, raw.at[0], weight_sem.at[3])
    region_load = pltpu.make_async_copy(region, reg_raw, weight_sem.at[4])
    loads = [
        pltpu.make_async_copy(hop, wn.at[pl.ds(0, 9)], weight_sem.at[0]),
        pltpu.make_async_copy(onsite, wn.at[pl.ds(9, 3)], weight_sem.at[1]),
        pltpu.make_async_copy(pair, wp, weight_sem.at[2]),
    ]
    first_load.start()
    region_load.start()
    for load in loads:
        load.start()
    region_load.wait()
    lane = lax.broadcasted_iota(jnp.int32, reg.shape, 1)
    row = jnp.zeros(reg.shape, jnp.float32)
    for xl in range(wide_len):
        for yl in range(row_len):
            value = reg_raw[xl : xl + 1, yl : yl + 1].astype(jnp.float32)
            row = jnp.where(lane == xl * row_len + yl, value, row)
    reg[...] = row
    first_load.wait()
    for xl in range(wide_len):
        wide_raw[:, xl * row_len : (xl + 1) * row_len] = raw[0, :, xl]
    r0[...] = wide_raw[...].astype(jnp.bfloat16)
    pl.semaphore_wait(barrier, sources - 1)

    for place, index in peers:
        pltpu.make_async_remote_copy(
            src_ref=reg, dst_ref=regs.at[me], send_sem=rsend_sem.at[0], recv_sem=rrecv_sem.at[0],
            device_id=place, device_id_type=MESH,
        ).start()

    for offset in (0, 2, 1):
        core, slot = offset // SLOTS, offset % SLOTS
        for dz in sorted(range(wide), key=lambda dz: -min(dz, wide - dz)):
            for dt in range(trans):
                to_z, to_t = lax.rem(z + dz, wide), lax.rem(t + dt, trans)
                v = (to_z * trans + to_t) * CHIP_VECTORS + offset
                copy = pltpu.make_async_remote_copy(
                    src_ref=r0.at[v], dst_ref=recv.at[slot, me], send_sem=send_sem.at[0], recv_sem=recv_sem.at[slot],
                    device_id=(group, to_z, to_t, jnp.int32(core)), device_id_type=MESH,
                )
                if dz or dt:
                    copy.start()
                else:
                    pl.when(c != core)(copy.start)

    regs[me] = reg[...]
    recv[0, me] = r0[my_first]

    @pl.when(c == 0)
    def _():
        recv[1, me] = r0[my_first + 1]

    buf[:, 0] = jnp.zeros((3,) + buf.shape[2:], buf.dtype)
    for load in loads:
        load.wait()
    for k in range(5):
        wpt[k] = wp[k].T

    lattice = lax.broadcasted_iota(jnp.int32, (cells, cells), 0)
    home = lax.broadcasted_iota(jnp.int32, (cells, cells), 1)
    to_lattice = (home_row(lattice, half, rows, wide_len, row_len) == home).astype(jnp.bfloat16)

    others = sources - 1

    def arrived(ref, sem):
        pltpu.make_async_copy(ref, ref, sem).wait()

    arrived(regs.at[pl.ds(0, others)], rrecv_sem.at[0])
    per = wide_len * row_len
    spots = lax.broadcasted_iota(jnp.int32, (cells, sources), 0)
    spots = home_row(spots, half, rows, wide_len, row_len)
    picks = (spots // per == lax.broadcasted_iota(jnp.int32, (cells, sources), 1)).astype(jnp.float32)
    spread = jnp.dot(picks, regs[...].reshape(sources, reg.shape[1]), preferred_element_type=jnp.float32)
    lanes = lax.broadcasted_iota(jnp.int32, spread.shape, 1)
    places = lax.broadcasted_iota(jnp.int32, spread.shape, 0)
    places = home_row(places, half, rows, wide_len, row_len) % per
    kinds = jnp.sum(jnp.where(lanes == places, spread, 0.0), axis=1, keepdims=True)
    kinds = jnp.broadcast_to(kinds, (cells, orbitals))
    for r in range(3):
        mask[r] = jnp.where(kinds == r, 1.0, 0.0).astype(jnp.bfloat16)

    def store_fields():
        field = current[...]
        y = lax.broadcasted_iota(jnp.int32, field.shape, 0) % rows
        below = jnp.where(y == 0, 0.0, pltpu.roll(field, 1, 0))
        above = jnp.where(y == rows - 1, 0.0, pltpu.roll(field, cells - 1, 0))
        for index, value in enumerate((below, field, above)):
            value = value.astype(jnp.bfloat16).reshape((half, 2, rows, orbitals))
            buf[index, 1 : half + 1] = value
            buf[index, half + 1, 0] = value[half - 1, 1]
            buf[index, half + 1, 1] = value[half - 1, 0]

    def send_home(which, slot, values):
        part = lax.dot_general(
            to_lattice, values, (((0,), (0,)), ((), ())), preferred_element_type=jnp.float32
        )
        stage[which, slot] = part.astype(jnp.bfloat16).reshape(stage.shape[2:])
        out[which, my_first + slot] = stage[which, slot, me]

        for place, index in peers:
            pltpu.make_async_remote_copy(
                src_ref=stage.at[which, slot, index], dst_ref=out.at[which, my_first + slot],
                send_sem=osend_sem.at[which, slot], recv_sem=orecv_sem.at[which],
                device_id=place, device_id_type=MESH,
            ).start()

    def slab(a, b):
        return buf[b + 1, 1 + a : 1 + a + half].reshape(cells, orbitals)

    def sector_slab(a, b, sector):
        return buf[b + 1, 1 + a : 1 + a + half, sector].reshape(cells // 2, orbitals)

    def apply(carry_scale, carry_old):
        normal = jnp.dot(slab(*HOP_OFFSETS[0]), wn[0], preferred_element_type=jnp.float32)
        for k in range(1, 9):
            normal = normal + jnp.dot(slab(*HOP_OFFSETS[k]), wn[k], preferred_element_type=jnp.float32)
        for r in range(3):
            chosen = slab(0, 0) * mask[r]
            normal = normal + jnp.dot(chosen, wn[9 + r], preferred_element_type=jnp.float32)
        to_e = jnp.zeros((cells // 2, orbitals), jnp.float32)
        to_h = jnp.zeros((cells // 2, orbitals), jnp.float32)
        for k, (a, b) in enumerate(PAIR_OFFSETS):
            to_e = to_e + jnp.dot(sector_slab(a, b, 1), wp[k], preferred_element_type=jnp.float32)
            to_h = to_h + jnp.dot(sector_slab(-a, -b, 0), wpt[k], preferred_element_type=jnp.float32)
        shape = (half, rows, orbitals)
        normal = normal.reshape(half, 2, rows, orbitals)
        new_e = normal[:, 0] + to_e.reshape(shape)
        new_h = to_h.reshape(shape) - normal[:, 1]
        new = jnp.stack([new_e, new_h], axis=1).reshape(cells, orbitals)
        new = carry_scale * new - carry_old * previous[...]
        previous[...] = current[...]
        current[...] = new

    def run(slot, carry):
        @pl.when(slot < my_slots)
        def _():
            arrived(recv.at[slot, pl.ds(0, others)], recv_sem.at[slot])
            current[...] = jnp.dot(
                to_lattice, recv[slot].reshape(cells, orbitals), preferred_element_type=jnp.float32
            )
            previous[...] = jnp.zeros(previous.shape, jnp.float32)

            def step(it, carry):
                store_fields()

                @pl.when(it == ITERS - 1)
                def _():
                    send_home(1, slot, slab(0, 0))

                first = it == 0
                apply(jnp.where(first, 1.0, 2.0), jnp.where(first, 0.0, 1.0))
                return carry

            lax.fori_loop(0, ITERS, step, 0)
            send_home(0, slot, current[...].astype(jnp.bfloat16))

        return carry

    lax.fori_loop(0, SLOTS, run, 0)

    for which, result in ((1, before), (0, last)):
        for core in range(sub):

            @pl.when(c == core)
            def _():
                arrived(out.at[which, pl.ds(0, count - SLOTS + core)], orecv_sem.at[which])

        wide_raw[...] = out[which].astype(jnp.float32)
        for xl in range(wide_len):
            raw[which, :, xl] = wide_raw[:, xl * row_len : (xl + 1) * row_len]
        pltpu.make_async_copy(raw.at[which], result, weight_sem.at[which]).start()

    for core in range(sub):

        @pl.when(c == core)
        def _():
            arrived(r0.at[pl.ds(0, count - SLOTS + core)], send_sem.at[0])

    arrived(regs.at[pl.ds(0, others)], rsend_sem.at[0])
    for slot in range(SLOTS):

        @pl.when(slot < my_slots)
        def _():
            for which in range(2):
                arrived(stage.at[which, slot, pl.ds(0, others)], osend_sem.at[which, slot])

    for which, result in ((1, before), (0, last)):
        pltpu.make_async_copy(raw.at[which], result, weight_sem.at[which]).wait()


def by_vectors(sizes, start_vectors, hopping, pairing, onsite, region):
    wide, trans, sub = sizes
    count, wide_len, row_len, orbitals = start_vectors.shape
    domains = trans * sub
    sources, per = wide * domains, wide_len * row_len
    half, rows = wide * wide_len // 2, domains * row_len
    cells = 2 * half * rows
    hbm = pl.BlockSpec(memory_space=pl.ANY)
    bf16, f32 = jnp.bfloat16, jnp.float32
    dma = pltpu.SemaphoreType.DMA
    return pl.pallas_call(
        functools.partial(vector_kernel, sizes + (wide_len, row_len)),
        out_shape=(jax.ShapeDtypeStruct(start_vectors.shape, f32),) * 2,
        in_specs=[hbm] * 5,
        out_specs=(hbm, hbm),
        scratch_shapes=[
            pltpu.VMEM((2,) + start_vectors.shape, f32),
            pltpu.VMEM((count, per, orbitals), f32),
            pltpu.VMEM((2, count, per, orbitals), bf16),
            pltpu.VMEM((count, per, orbitals), bf16),
            pltpu.VMEM(region.shape, region.dtype),
            pltpu.VMEM((1, 128), f32),
            pltpu.VMEM((SLOTS, sources, per, orbitals), bf16),
            pltpu.VMEM((sources, 1, 128), f32),
            pltpu.VMEM((12, orbitals, orbitals), bf16),
            pltpu.VMEM((5, orbitals, orbitals), bf16),
            pltpu.VMEM((5, orbitals, orbitals), bf16),
            pltpu.VMEM((3, half + 2, 2, rows, orbitals), bf16),
            pltpu.VMEM((cells, orbitals), f32),
            pltpu.VMEM((cells, orbitals), f32),
            pltpu.VMEM((2, SLOTS, sources, per, orbitals), bf16),
            pltpu.VMEM((3, cells, orbitals), bf16),
            dma((1,)),
            dma((SLOTS,)),
            dma((1,)),
            dma((1,)),
            dma((2, SLOTS)),
            dma((2,)),
            dma((5,)),
        ],
        compiler_params=pltpu.CompilerParams(
            collective_id=0, has_side_effects=True, vmem_limit_bytes=60 * 2**20
        ),
    )(start_vectors, region, hopping, pairing, onsite)


def solution(mesh):
    sizes = (mesh.shape["wide"], mesh.shape["trans"], mesh.shape["sub"])
    per_device = shards
    if sizes == (4, 2, 2):
        per_device = functools.partial(by_vectors, sizes)
    in_specs = (
        P(None, ("groups", "wide"), ("trans", "sub"), None),
        P(),
        P(),
        P(),
        P(("groups", "wide"), ("trans", "sub")),
    )
    out_specs = (
        P(None, ("groups", "wide"), ("trans", "sub"), None),
        P(None, ("groups", "wide"), ("trans", "sub"), None),
    )
    return jax.shard_map(per_device, mesh=mesh, in_specs=in_specs, out_specs=out_specs, check_vma=False)
```

```python
import functools

import jax
import jax.numpy as jnp
from jax import lax
from jax.experimental import pallas as pl
from jax.experimental.pallas import tpu as pltpu
from jax.sharding import PartitionSpec as P

MESH = pl.DeviceIdType.MESH

ITERS = 4


HOP_OFFSETS = [(-1, -1), (-1, 0), (-1, 1), (0, -1), (0, 0), (0, 1), (1, -1), (1, 0), (1, 1)]
PAIR_OFFSETS = [(0, 0), (1, 0), (-1, 0), (0, 1), (0, -1)]


def with_halo(array, sides, width):
    for axis, dim in sides:
        size, length = (lax.axis_size(axis), array.shape[dim])
        up = [(i, (i + 1) % size) for i in range(size - 1)]
        down = [(j, i) for i, j in up]
        last = lax.slice_in_dim(array, length - width, length, axis=dim)
        leading = lax.slice_in_dim(array, 0, width, axis=dim)
        before = lax.ppermute(last, axis, up)
        after = lax.ppermute(leading, axis, down)
        array = jnp.concatenate([before, array, after], axis=dim)
    return array


def swapped(value, axis, bit):
    mask = 2**bit
    pairs = [(source, source ^ mask) for source in range(lax.axis_size(axis))]
    return lax.ppermute(value, axis, pairs)


def block_product(slab, matrix):
    return jnp.einsum("vxyb,bc->vxyc", slab, matrix, preferred_element_type=jnp.float32)


def shards(start_vectors, hopping, pairing, onsite, region):
    vectors, count_x, count_y, orbitals = start_vectors.shape
    wide_index = lax.axis_index("wide")
    wide_count = lax.axis_size("wide")
    half_size = wide_count // 2
    bit_count = wide_count.bit_length() - 1
    electron = wide_index < half_size
    sector_sign = jnp.where(electron, 1, -1).astype(jnp.int32)
    sector_scale = jnp.where(electron, 1.0, -1.0).astype(jnp.float32)
    pair_used = jnp.where(electron, pairing, jnp.swapaxes(pairing, 1, 2))
    kinds = jnp.arange(onsite.shape[0], dtype=jnp.int32)
    chosen = (region[None, :, :] == kinds[:, None, None]).astype(jnp.bfloat16)
    onsite_blocks = jnp.sum(chosen[:, :, :, None, None] * onsite[:, None, None, :, :], axis=0)
    anchor = jnp.int32(0)

    def window(padded, start_x, start_y):
        starts = (anchor, jnp.asarray(start_x, jnp.int32), jnp.asarray(start_y, jnp.int32), anchor)
        return lax.dynamic_slice(padded, starts, (vectors, count_x, count_y, orbitals))

    def apply_hamiltonian(rounded):
        padded = with_halo(rounded, (("wide", 1), (("trans", "sub"), 2)), 1)
        received = padded
        for bit_index in range(bit_count):
            received = swapped(received, "wide", bit_index)
        partner = jnp.flip(received, 1)
        normal = jnp.einsum(
            "vxyb,xybc->vxyc", rounded, onsite_blocks, preferred_element_type=jnp.float32
        )
        for offset_index, (shift_x, shift_y) in enumerate(HOP_OFFSETS):
            slab = window(padded, 1 + sector_sign * shift_x, 1 + shift_y)
            normal = normal + block_product(slab, hopping[offset_index])
        paired = jnp.zeros(rounded.shape, jnp.float32)
        for offset_index, (shift_x, shift_y) in enumerate(PAIR_OFFSETS):
            slab = window(partner, 1 + shift_x, 1 + sector_sign * shift_y)
            paired = paired + block_product(slab, pair_used[offset_index])
        return sector_scale * normal + paired

    previous = start_vectors
    current = apply_hamiltonian(start_vectors.astype(jnp.bfloat16))
    for step in range(ITERS - 1):
        following = 2.0 * apply_hamiltonian(current.astype(jnp.bfloat16)) - previous
        previous = current
        current = following
    return (current, previous)


CHIP_VECTORS = 3
SLOTS = 2


def home_row(out_row, half, rows, wide_len, row_len):
    x = out_row // (2 * rows)
    sector = (out_row // rows) % 2
    y = out_row % rows
    column = jnp.where(sector == 0, x, 2 * half - 1 - x)
    domains = rows // row_len
    return ((column // wide_len) * domains + y // row_len) * (wide_len * row_len) + (column % wide_len) * row_len + y % row_len


def vector_kernel(
    sizes, start, region, hop, pair, onsite, results,
    raw, wide_raw, final, out, r0, reg_raw, reg, recv, regs, wn, wp, wpt, buf, previous, current, stage, mask,
    send_sem, recv_sem, rsend_sem, rrecv_sem, osend_sem, orecv_sem, weight_sem,
):
    wide, trans, sub, wide_len, row_len = sizes
    domains = trans * sub
    sources = wide * domains
    half = wide * wide_len // 2
    rows = domains * row_len
    cells = 2 * half * rows
    count, orbitals = r0.shape[0], r0.shape[2]
    group = lax.axis_index("groups")
    z, t, c = lax.axis_index("wide"), lax.axis_index("trans"), lax.axis_index("sub")
    me = z * domains + t * sub + c
    my_first = (z * trans + t) * CHIP_VECTORS + c * SLOTS
    my_slots = SLOTS - c

    peers = []
    for dz in sorted(range(wide), key=lambda dz: -min(dz, wide - dz)):
        for dt in range(trans):
            for dc in range(sub):
                if dz or dt or dc:
                    to_z, to_t, to_c = lax.rem(z + dz, wide), lax.rem(t + dt, trans), lax.rem(c + dc, sub)
                    peers.append(((group, to_z, to_t, to_c), to_z * domains + to_t * sub + to_c))

    barrier = pltpu.get_barrier_semaphore()

    for place, index in peers:
        pl.semaphore_signal(barrier, inc=1, device_id=place, device_id_type=MESH)

    first_load = pltpu.make_async_copy(start, raw, weight_sem.at[3])
    region_load = pltpu.make_async_copy(region, reg_raw, weight_sem.at[4])
    loads = [
        pltpu.make_async_copy(hop, wn.at[pl.ds(0, 9)], weight_sem.at[0]),
        pltpu.make_async_copy(onsite, wn.at[pl.ds(9, 3)], weight_sem.at[1]),
        pltpu.make_async_copy(pair, wp, weight_sem.at[2]),
    ]
    first_load.start()
    region_load.start()
    for load in loads:
        load.start()
    region_load.wait()
    lane = lax.broadcasted_iota(jnp.int32, reg.shape, 1)
    row = jnp.zeros(reg.shape, jnp.float32)
    for xl in range(wide_len):
        for yl in range(row_len):
            value = reg_raw[xl : xl + 1, yl : yl + 1].astype(jnp.float32)
            row = jnp.where(lane == xl * row_len + yl, value, row)
    reg[...] = row
    first_load.wait()
    for xl in range(wide_len):
        wide_raw[:, xl * row_len : (xl + 1) * row_len] = raw[:, xl]
    r0[...] = wide_raw[...].astype(jnp.bfloat16)
    pl.semaphore_wait(barrier, sources - 1)

    for place, index in peers:
        pltpu.make_async_remote_copy(
            src_ref=reg, dst_ref=regs.at[me], send_sem=rsend_sem.at[0], recv_sem=rrecv_sem.at[0],
            device_id=place, device_id_type=MESH,
        ).start()

    for offset in (0, 2, 1):
        core, slot = offset // SLOTS, offset % SLOTS
        for dz in sorted(range(wide), key=lambda dz: -min(dz, wide - dz)):
            for dt in range(trans):
                to_z, to_t = lax.rem(z + dz, wide), lax.rem(t + dt, trans)
                v = (to_z * trans + to_t) * CHIP_VECTORS + offset
                copy = pltpu.make_async_remote_copy(
                    src_ref=r0.at[v], dst_ref=recv.at[slot, me], send_sem=send_sem.at[0], recv_sem=recv_sem.at[slot],
                    device_id=(group, to_z, to_t, jnp.int32(core)), device_id_type=MESH,
                )
                if dz or dt:
                    copy.start()
                else:
                    pl.when(c != core)(copy.start)

    regs[me] = reg[...]
    recv[0, me] = r0[my_first]

    @pl.when(c == 0)
    def _():
        recv[1, me] = r0[my_first + 1]

    buf[:, 0] = jnp.zeros((3,) + buf.shape[2:], buf.dtype)
    for load in loads:
        load.wait()
    for k in range(5):
        wpt[k] = wp[k].T

    lattice = lax.broadcasted_iota(jnp.int32, (cells, cells), 0)
    home = lax.broadcasted_iota(jnp.int32, (cells, cells), 1)
    to_lattice = (home_row(lattice, half, rows, wide_len, row_len) == home).astype(jnp.bfloat16)

    others = sources - 1

    def arrived(ref, sem):
        pltpu.make_async_copy(ref, ref, sem).wait()

    arrived(regs.at[pl.ds(0, others)], rrecv_sem.at[0])
    per = wide_len * row_len
    spots = lax.broadcasted_iota(jnp.int32, (cells, sources), 0)
    spots = home_row(spots, half, rows, wide_len, row_len)
    picks = (spots // per == lax.broadcasted_iota(jnp.int32, (cells, sources), 1)).astype(jnp.float32)
    spread = jnp.dot(picks, regs[...].reshape(sources, reg.shape[1]), preferred_element_type=jnp.float32)
    lanes = lax.broadcasted_iota(jnp.int32, spread.shape, 1)
    places = lax.broadcasted_iota(jnp.int32, spread.shape, 0)
    places = home_row(places, half, rows, wide_len, row_len) % per
    kinds = jnp.sum(jnp.where(lanes == places, spread, 0.0), axis=1, keepdims=True)
    kinds = jnp.broadcast_to(kinds, (cells, orbitals))
    for r in range(3):
        mask[r] = jnp.where(kinds == r, 1.0, 0.0).astype(jnp.bfloat16)

    def store_fields():
        field = current[...]
        y = lax.broadcasted_iota(jnp.int32, field.shape, 0) % rows
        below = jnp.where(y == 0, 0.0, pltpu.roll(field, 1, 0))
        above = jnp.where(y == rows - 1, 0.0, pltpu.roll(field, cells - 1, 0))
        for index, value in enumerate((below, field, above)):
            value = value.astype(jnp.bfloat16).reshape((half, 2, rows, orbitals))
            buf[index, 1 : half + 1] = value
            buf[index, half + 1, 0] = value[half - 1, 1]
            buf[index, half + 1, 1] = value[half - 1, 0]

    def send_home(which, slot, values):
        part = lax.dot_general(
            to_lattice, values, (((0,), (0,)), ((), ())), preferred_element_type=jnp.float32
        )
        stage[which, slot] = part.astype(jnp.bfloat16).reshape(stage.shape[2:])
        out[which, my_first + slot] = stage[which, slot, me]

        for place, index in peers:
            pltpu.make_async_remote_copy(
                src_ref=stage.at[which, slot, index], dst_ref=out.at[which, my_first + slot],
                send_sem=osend_sem.at[which, slot], recv_sem=orecv_sem.at[which],
                device_id=place, device_id_type=MESH,
            ).start()

    def slab(a, b):
        return buf[b + 1, 1 + a : 1 + a + half].reshape(cells, orbitals)

    def sector_slab(a, b, sector):
        return buf[b + 1, 1 + a : 1 + a + half, sector].reshape(cells // 2, orbitals)

    def apply(carry_scale, carry_old):
        normal_slabs = [slab(a, b) for a, b in HOP_OFFSETS] + [slab(0, 0) * mask[r] for r in range(3)]
        normal = jnp.dot(
            jnp.concatenate(normal_slabs, axis=1), wn[...].reshape(12 * orbitals, orbitals),
            preferred_element_type=jnp.float32,
        )
        to_e = jnp.dot(
            jnp.concatenate([sector_slab(a, b, 1) for a, b in PAIR_OFFSETS], axis=1),
            wp[...].reshape(5 * orbitals, orbitals), preferred_element_type=jnp.float32,
        )
        to_h = jnp.dot(
            jnp.concatenate([sector_slab(-a, -b, 0) for a, b in PAIR_OFFSETS], axis=1),
            wpt[...].reshape(5 * orbitals, orbitals), preferred_element_type=jnp.float32,
        )
        shape = (half, rows, orbitals)
        normal = normal.reshape(half, 2, rows, orbitals)
        new_e = normal[:, 0] + to_e.reshape(shape)
        new_h = to_h.reshape(shape) - normal[:, 1]
        new = jnp.stack([new_e, new_h], axis=1).reshape(cells, orbitals)
        new = carry_scale * new - carry_old * previous[...]
        previous[...] = current[...]
        current[...] = new

    def run(slot, carry):
        @pl.when(slot < my_slots)
        def _():
            arrived(recv.at[slot, pl.ds(0, others)], recv_sem.at[slot])
            current[...] = jnp.dot(
                to_lattice, recv[slot].reshape(cells, orbitals), preferred_element_type=jnp.float32
            )
            previous[...] = jnp.zeros(previous.shape, jnp.float32)

            def step(it, carry):
                store_fields()

                @pl.when(it == ITERS - 1)
                def _():
                    send_home(1, slot, slab(0, 0))

                first = it == 0
                apply(jnp.where(first, 1.0, 2.0), jnp.where(first, 0.0, 1.0))
                return carry

            lax.fori_loop(0, ITERS, step, 0)
            send_home(0, slot, current[...].astype(jnp.bfloat16))

        return carry

    lax.fori_loop(0, SLOTS, run, 0)

    for which in (1, 0):
        for core in range(sub):

            @pl.when(c == core)
            def _():
                arrived(out.at[which, pl.ds(0, count - SLOTS + core)], orecv_sem.at[which])

        wide_raw[...] = out[which].astype(jnp.float32)
        for xl in range(wide_len):
            final[which, :, xl] = wide_raw[:, xl * row_len : (xl + 1) * row_len].astype(jnp.bfloat16)
        pltpu.make_async_copy(final.at[which], results.at[which], weight_sem.at[which]).start()

    for core in range(sub):

        @pl.when(c == core)
        def _():
            arrived(r0.at[pl.ds(0, count - SLOTS + core)], send_sem.at[0])

    arrived(regs.at[pl.ds(0, others)], rsend_sem.at[0])
    for slot in range(SLOTS):

        @pl.when(slot < my_slots)
        def _():
            for which in range(2):
                arrived(stage.at[which, slot, pl.ds(0, others)], osend_sem.at[which, slot])

    for which in (1, 0):
        pltpu.make_async_copy(final.at[which], results.at[which], weight_sem.at[which]).wait()


def by_vectors(sizes, start_vectors, hopping, pairing, onsite, region):
    wide, trans, sub = sizes
    count, wide_len, row_len, orbitals = start_vectors.shape
    domains = trans * sub
    sources, per = wide * domains, wide_len * row_len
    half, rows = wide * wide_len // 2, domains * row_len
    cells = 2 * half * rows
    hbm = pl.BlockSpec(memory_space=pl.ANY)
    bf16, f32 = jnp.bfloat16, jnp.float32
    dma = pltpu.SemaphoreType.DMA
    results = pl.pallas_call(
        functools.partial(vector_kernel, sizes + (wide_len, row_len)),
        out_shape=jax.ShapeDtypeStruct((2,) + start_vectors.shape, bf16),
        in_specs=[hbm] * 5,
        out_specs=hbm,
        scratch_shapes=[
            pltpu.VMEM(start_vectors.shape, f32),
            pltpu.VMEM((count, per, orbitals), f32),
            pltpu.VMEM((2,) + start_vectors.shape, bf16),
            pltpu.VMEM((2, count, per, orbitals), bf16),
            pltpu.VMEM((count, per, orbitals), bf16),
            pltpu.VMEM(region.shape, region.dtype),
            pltpu.VMEM((1, 128), f32),
            pltpu.VMEM((SLOTS, sources, per, orbitals), bf16),
            pltpu.VMEM((sources, 1, 128), f32),
            pltpu.VMEM((12, orbitals, orbitals), bf16),
            pltpu.VMEM((5, orbitals, orbitals), bf16),
            pltpu.VMEM((5, orbitals, orbitals), bf16),
            pltpu.VMEM((3, half + 2, 2, rows, orbitals), bf16),
            pltpu.VMEM((cells, orbitals), f32),
            pltpu.VMEM((cells, orbitals), f32),
            pltpu.VMEM((2, SLOTS, sources, per, orbitals), bf16),
            pltpu.VMEM((3, cells, orbitals), bf16),
            dma((1,)),
            dma((SLOTS,)),
            dma((1,)),
            dma((1,)),
            dma((2, SLOTS)),
            dma((2,)),
            dma((5,)),
        ],
        compiler_params=pltpu.CompilerParams(
            collective_id=0, has_side_effects=True, vmem_limit_bytes=60 * 2**20
        ),
    )(start_vectors, region, hopping, pairing, onsite)
    return results[0].astype(f32), results[1].astype(f32)


def solution(mesh):
    sizes = (mesh.shape["wide"], mesh.shape["trans"], mesh.shape["sub"])
    per_device = shards
    if sizes == (4, 2, 2):
        per_device = functools.partial(by_vectors, sizes)
    in_specs = (
        P(None, ("groups", "wide"), ("trans", "sub"), None),
        P(),
        P(),
        P(),
        P(("groups", "wide"), ("trans", "sub")),
    )
    out_specs = (
        P(None, ("groups", "wide"), ("trans", "sub"), None),
        P(None, ("groups", "wide"), ("trans", "sub"), None),
    )
    return jax.shard_map(per_device, mesh=mesh, in_specs=in_specs, out_specs=out_specs, check_vma=False)
```

```python
import functools

import jax
import jax.numpy as jnp
from jax import lax
from jax.experimental import pallas as pl
from jax.experimental.pallas import tpu as pltpu
from jax.sharding import PartitionSpec as P

MESH = pl.DeviceIdType.MESH

ITERS = 4


HOP_OFFSETS = [(-1, -1), (-1, 0), (-1, 1), (0, -1), (0, 0), (0, 1), (1, -1), (1, 0), (1, 1)]
PAIR_OFFSETS = [(0, 0), (1, 0), (-1, 0), (0, 1), (0, -1)]


def with_halo(array, sides, width):
    for axis, dim in sides:
        size, length = (lax.axis_size(axis), array.shape[dim])
        up = [(i, (i + 1) % size) for i in range(size - 1)]
        down = [(j, i) for i, j in up]
        last = lax.slice_in_dim(array, length - width, length, axis=dim)
        leading = lax.slice_in_dim(array, 0, width, axis=dim)
        before = lax.ppermute(last, axis, up)
        after = lax.ppermute(leading, axis, down)
        array = jnp.concatenate([before, array, after], axis=dim)
    return array


def swapped(value, axis, bit):
    mask = 2**bit
    pairs = [(source, source ^ mask) for source in range(lax.axis_size(axis))]
    return lax.ppermute(value, axis, pairs)


def block_product(slab, matrix):
    return jnp.einsum("vxyb,bc->vxyc", slab, matrix, preferred_element_type=jnp.float32)


def shards(start_vectors, hopping, pairing, onsite, region):
    vectors, count_x, count_y, orbitals = start_vectors.shape
    wide_index = lax.axis_index("wide")
    wide_count = lax.axis_size("wide")
    half_size = wide_count // 2
    bit_count = wide_count.bit_length() - 1
    electron = wide_index < half_size
    sector_sign = jnp.where(electron, 1, -1).astype(jnp.int32)
    sector_scale = jnp.where(electron, 1.0, -1.0).astype(jnp.float32)
    pair_used = jnp.where(electron, pairing, jnp.swapaxes(pairing, 1, 2))
    kinds = jnp.arange(onsite.shape[0], dtype=jnp.int32)
    chosen = (region[None, :, :] == kinds[:, None, None]).astype(jnp.bfloat16)
    onsite_blocks = jnp.sum(chosen[:, :, :, None, None] * onsite[:, None, None, :, :], axis=0)
    anchor = jnp.int32(0)

    def window(padded, start_x, start_y):
        starts = (anchor, jnp.asarray(start_x, jnp.int32), jnp.asarray(start_y, jnp.int32), anchor)
        return lax.dynamic_slice(padded, starts, (vectors, count_x, count_y, orbitals))

    def apply_hamiltonian(rounded):
        padded = with_halo(rounded, (("wide", 1), (("trans", "sub"), 2)), 1)
        received = padded
        for bit_index in range(bit_count):
            received = swapped(received, "wide", bit_index)
        partner = jnp.flip(received, 1)
        normal = jnp.einsum(
            "vxyb,xybc->vxyc", rounded, onsite_blocks, preferred_element_type=jnp.float32
        )
        for offset_index, (shift_x, shift_y) in enumerate(HOP_OFFSETS):
            slab = window(padded, 1 + sector_sign * shift_x, 1 + shift_y)
            normal = normal + block_product(slab, hopping[offset_index])
        paired = jnp.zeros(rounded.shape, jnp.float32)
        for offset_index, (shift_x, shift_y) in enumerate(PAIR_OFFSETS):
            slab = window(partner, 1 + shift_x, 1 + sector_sign * shift_y)
            paired = paired + block_product(slab, pair_used[offset_index])
        return sector_scale * normal + paired

    previous = start_vectors
    current = apply_hamiltonian(start_vectors.astype(jnp.bfloat16))
    for step in range(ITERS - 1):
        following = 2.0 * apply_hamiltonian(current.astype(jnp.bfloat16)) - previous
        previous = current
        current = following
    return (current, previous)


CHIP_VECTORS = 3
SLOTS = 2


def home_row(out_row, half, rows, wide_len, row_len):
    x = out_row // (2 * rows)
    sector = (out_row // rows) % 2
    y = out_row % rows
    column = jnp.where(sector == 0, x, 2 * half - 1 - x)
    domains = rows // row_len
    return ((column // wide_len) * domains + y // row_len) * (wide_len * row_len) + (column % wide_len) * row_len + y % row_len


def vector_kernel(
    sizes, start, region, hop, pair, onsite, results,
    raw, wide_raw, final, out, r0, reg_raw, reg, recv, regs, wn, wp, wpt, buf, previous, current, stage, mask,
    send_sem, recv_sem, rsend_sem, rrecv_sem, osend_sem, orecv_sem, weight_sem,
):
    wide, trans, sub, wide_len, row_len = sizes
    domains = trans * sub
    sources = wide * domains
    half = wide * wide_len // 2
    rows = domains * row_len
    cells = 2 * half * rows
    count, orbitals = r0.shape[0], r0.shape[2]
    group = lax.axis_index("groups")
    z, t, c = lax.axis_index("wide"), lax.axis_index("trans"), lax.axis_index("sub")
    me = z * domains + t * sub + c
    my_first = (z * trans + t) * CHIP_VECTORS + c * SLOTS
    my_slots = SLOTS - c

    peers = []
    for dz in sorted(range(wide), key=lambda dz: -min(dz, wide - dz)):
        for dt in range(trans):
            for dc in range(sub):
                if dz or dt or dc:
                    to_z, to_t, to_c = lax.rem(z + dz, wide), lax.rem(t + dt, trans), lax.rem(c + dc, sub)
                    peers.append(((group, to_z, to_t, to_c), to_z * domains + to_t * sub + to_c))

    barrier = pltpu.get_barrier_semaphore()

    for place, index in peers:
        pl.semaphore_signal(barrier, inc=1, device_id=place, device_id_type=MESH)

    first_load = pltpu.make_async_copy(start, raw, weight_sem.at[3])
    region_load = pltpu.make_async_copy(region, reg_raw, weight_sem.at[4])
    loads = [
        pltpu.make_async_copy(hop, wn.at[pl.ds(0, 9)], weight_sem.at[0]),
        pltpu.make_async_copy(onsite, wn.at[pl.ds(9, 3)], weight_sem.at[1]),
        pltpu.make_async_copy(pair, wp, weight_sem.at[2]),
    ]
    first_load.start()
    region_load.start()
    for load in loads:
        load.start()
    region_load.wait()
    lane = lax.broadcasted_iota(jnp.int32, reg.shape, 1)
    row = jnp.zeros(reg.shape, jnp.float32)
    for xl in range(wide_len):
        for yl in range(row_len):
            value = reg_raw[xl : xl + 1, yl : yl + 1].astype(jnp.float32)
            row = jnp.where(lane == xl * row_len + yl, value, row)
    reg[...] = row
    first_load.wait()
    for xl in range(wide_len):
        wide_raw[:, xl * row_len : (xl + 1) * row_len] = raw[:, xl]
    r0[...] = wide_raw[...].astype(jnp.bfloat16)
    pl.semaphore_wait(barrier, sources - 1)

    for place, index in peers:
        pltpu.make_async_remote_copy(
            src_ref=reg, dst_ref=regs.at[me], send_sem=rsend_sem.at[0], recv_sem=rrecv_sem.at[0],
            device_id=place, device_id_type=MESH,
        ).start()

    for offset in (0, 2, 1):
        core, slot = offset // SLOTS, offset % SLOTS
        for dz in sorted(range(wide), key=lambda dz: -min(dz, wide - dz)):
            for dt in range(trans):
                to_z, to_t = lax.rem(z + dz, wide), lax.rem(t + dt, trans)
                v = (to_z * trans + to_t) * CHIP_VECTORS + offset
                copy = pltpu.make_async_remote_copy(
                    src_ref=r0.at[v], dst_ref=recv.at[slot, me], send_sem=send_sem.at[0], recv_sem=recv_sem.at[slot],
                    device_id=(group, to_z, to_t, jnp.int32(core)), device_id_type=MESH,
                )
                if dz or dt:
                    copy.start()
                else:
                    pl.when(c != core)(copy.start)

    regs[me] = reg[...]
    recv[0, me] = r0[my_first]

    @pl.when(c == 0)
    def _():
        recv[1, me] = r0[my_first + 1]

    buf[:, 0] = jnp.zeros((3,) + buf.shape[2:], buf.dtype)
    for load in loads:
        load.wait()
    for k in range(5):
        wpt[k] = wp[k].T

    lattice = lax.broadcasted_iota(jnp.int32, (cells, cells), 0)
    home = lax.broadcasted_iota(jnp.int32, (cells, cells), 1)
    to_lattice = (home_row(lattice, half, rows, wide_len, row_len) == home).astype(jnp.bfloat16)

    others = sources - 1

    def arrived(ref, sem):
        pltpu.make_async_copy(ref, ref, sem).wait()

    arrived(regs.at[pl.ds(0, others)], rrecv_sem.at[0])
    per = wide_len * row_len
    spots = lax.broadcasted_iota(jnp.int32, (cells, sources), 0)
    spots = home_row(spots, half, rows, wide_len, row_len)
    picks = (spots // per == lax.broadcasted_iota(jnp.int32, (cells, sources), 1)).astype(jnp.float32)
    spread = jnp.dot(picks, regs[...].reshape(sources, reg.shape[1]), preferred_element_type=jnp.float32)
    lanes = lax.broadcasted_iota(jnp.int32, spread.shape, 1)
    places = lax.broadcasted_iota(jnp.int32, spread.shape, 0)
    places = home_row(places, half, rows, wide_len, row_len) % per
    kinds = jnp.sum(jnp.where(lanes == places, spread, 0.0), axis=1, keepdims=True)
    kinds = jnp.broadcast_to(kinds, (cells, orbitals))
    for r in range(3):
        mask[r] = jnp.where(kinds == r, 1.0, 0.0).astype(jnp.bfloat16)

    def store_fields():
        field = current[...]
        y = lax.broadcasted_iota(jnp.int32, field.shape, 0) % rows
        below = jnp.where(y == 0, 0.0, pltpu.roll(field, 1, 0))
        above = jnp.where(y == rows - 1, 0.0, pltpu.roll(field, cells - 1, 0))
        for index, value in enumerate((below, field, above)):
            value = value.astype(jnp.bfloat16).reshape((half, 2, rows, orbitals))
            buf[index, 1 : half + 1] = value
            buf[index, half + 1, 0] = value[half - 1, 1]
            buf[index, half + 1, 1] = value[half - 1, 0]

    def send_home(which, slot, values):
        part = lax.dot_general(
            to_lattice, values, (((0,), (0,)), ((), ())), preferred_element_type=jnp.float32
        )
        stage[which, slot] = part.astype(jnp.bfloat16).reshape(stage.shape[2:])
        out[which, my_first + slot] = stage[which, slot, me]

        for place, index in peers:
            pltpu.make_async_remote_copy(
                src_ref=stage.at[which, slot, index], dst_ref=out.at[which, my_first + slot],
                send_sem=osend_sem.at[which, slot], recv_sem=orecv_sem.at[which],
                device_id=place, device_id_type=MESH,
            ).start()

    def slab(a, b):
        return buf[b + 1, 1 + a : 1 + a + half].reshape(cells, orbitals)

    def sector_slab(a, b, sector):
        return buf[b + 1, 1 + a : 1 + a + half, sector].reshape(cells // 2, orbitals)

    def apply(carry_scale, carry_old):
        normal_slabs = [slab(a, b) for a, b in HOP_OFFSETS] + [slab(0, 0) * mask[r] for r in range(3)]
        normal = jnp.dot(
            jnp.concatenate(normal_slabs, axis=1), wn[...].reshape(12 * orbitals, orbitals),
            preferred_element_type=jnp.float32,
        )
        to_e = jnp.dot(
            jnp.concatenate([sector_slab(a, b, 1) for a, b in PAIR_OFFSETS], axis=1),
            wp[...].reshape(5 * orbitals, orbitals), preferred_element_type=jnp.float32,
        )
        to_h = jnp.dot(
            jnp.concatenate([sector_slab(-a, -b, 0) for a, b in PAIR_OFFSETS], axis=1),
            wpt[...].reshape(5 * orbitals, orbitals), preferred_element_type=jnp.float32,
        )
        shape = (half, rows, orbitals)
        normal = normal.reshape(half, 2, rows, orbitals)
        new_e = normal[:, 0] + to_e.reshape(shape)
        new_h = to_h.reshape(shape) - normal[:, 1]
        new = jnp.stack([new_e, new_h], axis=1).reshape(cells, orbitals)
        new = carry_scale * new - carry_old * previous[...]
        previous[...] = current[...]
        current[...] = new

    def run(slot, carry):
        @pl.when(slot < my_slots)
        def _():
            arrived(recv.at[slot, pl.ds(0, others)], recv_sem.at[slot])
            current[...] = jnp.dot(
                to_lattice, recv[slot].reshape(cells, orbitals), preferred_element_type=jnp.float32
            )
            previous[...] = jnp.zeros(previous.shape, jnp.float32)

            def step(it, carry):
                store_fields()

                @pl.when(it == ITERS - 1)
                def _():
                    send_home(1, slot, slab(0, 0))

                first = it == 0
                apply(jnp.where(first, 1.0, 2.0), jnp.where(first, 0.0, 1.0))
                return carry

            lax.fori_loop(0, ITERS, step, 0)
            send_home(0, slot, current[...].astype(jnp.bfloat16))

        return carry

    lax.fori_loop(0, SLOTS, run, 0)

    for which in (1, 0):
        for core in range(sub):

            @pl.when(c == core)
            def _():
                arrived(out.at[which, pl.ds(0, count - SLOTS + core)], orecv_sem.at[which])

        arrivals = out[which].astype(jnp.float32)
        for xl in range(wide_len):
            final[which, :, xl] = arrivals[:, xl * row_len : (xl + 1) * row_len].astype(jnp.bfloat16)
        pltpu.make_async_copy(final.at[which], results.at[which], weight_sem.at[which]).start()

    for core in range(sub):

        @pl.when(c == core)
        def _():
            arrived(r0.at[pl.ds(0, count - SLOTS + core)], send_sem.at[0])

    arrived(regs.at[pl.ds(0, others)], rsend_sem.at[0])
    for slot in range(SLOTS):

        @pl.when(slot < my_slots)
        def _():
            for which in range(2):
                arrived(stage.at[which, slot, pl.ds(0, others)], osend_sem.at[which, slot])

    for which in (1, 0):
        pltpu.make_async_copy(final.at[which], results.at[which], weight_sem.at[which]).wait()


def by_vectors(sizes, start_vectors, hopping, pairing, onsite, region):
    wide, trans, sub = sizes
    count, wide_len, row_len, orbitals = start_vectors.shape
    domains = trans * sub
    sources, per = wide * domains, wide_len * row_len
    half, rows = wide * wide_len // 2, domains * row_len
    cells = 2 * half * rows
    hbm = pl.BlockSpec(memory_space=pl.ANY)
    bf16, f32 = jnp.bfloat16, jnp.float32
    dma = pltpu.SemaphoreType.DMA
    results = pl.pallas_call(
        functools.partial(vector_kernel, sizes + (wide_len, row_len)),
        out_shape=jax.ShapeDtypeStruct((2,) + start_vectors.shape, bf16),
        in_specs=[hbm] * 5,
        out_specs=hbm,
        scratch_shapes=[
            pltpu.VMEM(start_vectors.shape, f32),
            pltpu.VMEM((count, per, orbitals), f32),
            pltpu.VMEM((2,) + start_vectors.shape, bf16),
            pltpu.VMEM((2, count, per, orbitals), bf16),
            pltpu.VMEM((count, per, orbitals), bf16),
            pltpu.VMEM(region.shape, region.dtype),
            pltpu.VMEM((1, 128), f32),
            pltpu.VMEM((SLOTS, sources, per, orbitals), bf16),
            pltpu.VMEM((sources, 1, 128), f32),
            pltpu.VMEM((12, orbitals, orbitals), bf16),
            pltpu.VMEM((5, orbitals, orbitals), bf16),
            pltpu.VMEM((5, orbitals, orbitals), bf16),
            pltpu.VMEM((3, half + 2, 2, rows, orbitals), bf16),
            pltpu.VMEM((cells, orbitals), f32),
            pltpu.VMEM((cells, orbitals), f32),
            pltpu.VMEM((2, SLOTS, sources, per, orbitals), bf16),
            pltpu.VMEM((3, cells, orbitals), bf16),
            dma((1,)),
            dma((SLOTS,)),
            dma((1,)),
            dma((1,)),
            dma((2, SLOTS)),
            dma((2,)),
            dma((5,)),
        ],
        compiler_params=pltpu.CompilerParams(
            collective_id=0, has_side_effects=True, vmem_limit_bytes=60 * 2**20
        ),
    )(start_vectors, region, hopping, pairing, onsite)
    return results[0].astype(f32), results[1].astype(f32)


def solution(mesh):
    sizes = (mesh.shape["wide"], mesh.shape["trans"], mesh.shape["sub"])
    per_device = shards
    if sizes == (4, 2, 2):
        per_device = functools.partial(by_vectors, sizes)
    in_specs = (
        P(None, ("groups", "wide"), ("trans", "sub"), None),
        P(),
        P(),
        P(),
        P(("groups", "wide"), ("trans", "sub")),
    )
    out_specs = (
        P(None, ("groups", "wide"), ("trans", "sub"), None),
        P(None, ("groups", "wide"), ("trans", "sub"), None),
    )
    return jax.shard_map(per_device, mesh=mesh, in_specs=in_specs, out_specs=out_specs, check_vma=False)
```
